512 devices in a mesh: mem: 16 (over y, core), tile: 32 (over z, x).
Axes of the slice: x: 4, y: 8, z: 8, core: 2. Of those that a mesh axis runs over, the one named last changes fastest.
Arguments:
- ensemble_profiles_before: bfloat16 [64, 40, 65536], P('mem', None, 'tile'), may hold values from -6 to 6
- mixing_coefficient: float32 [65536], P('tile'), may hold values from 0.05 to 0.24
- surface_driver: float32 [64, 65536], P('mem', 'tile'), may hold values from -3 to 3
- terrain_indicator: int32 [65536], P('tile'), may hold values 0 or 1
- measured_profile_position: int32 [131072], P('tile'), may hold values from 0 to 2047
- measured_field_index: int32 [131072], P('tile'), may hold values from 0 to 39
- obs_valid: int32 [131072], P('tile'), may hold values 0 or 1
- obs_value: bfloat16 [131072], P('tile'), may hold values from -6 to 6
- obs_error: bfloat16 [131072], P('tile'), may hold values from 0.5 to 4
- local_weight: float32 [16, 32, 20480], P('mem', 'tile'), may hold values from 0.001 to 0.03
Outputs:
- analysis: bfloat16 [64, 40, 65536], P('mem', None, 'tile')
The draws below stay inside these ranges and needn't reach their ends.
All inputs are finite; a program needn't handle non-finite values. No bound on the sum of `terrain_indicator` or of `obs_valid` on one device may be relied on, other than what follows from the above.
Results may differ from the reference program's by a relative error of at most 0.0034.
Values may be sent and summed in bfloat16 or wider, within the bound.
No kernel may reach another device: no remote copies, remote signals or barrier semaphores. Data moves between devices by JAX's collectives and lax.ppermute only.
A program may use at most 64 MiB of HBM per device.

```python
import math
import jax
import jax.numpy as jnp
from jax import lax

K = 64
PROFILE_SIZE = 40
BLK = 128
OBS_T = 4096
REACH = 2
NS_ITERS = 3
C_TILE = 2048
COLS = 65536
NB_TILE = 16
P_OBS = 20480
N_TILE = 32


def set_ends(values, stream_key, least, largest):
    longest = values.shape.index(max(values.shape))
    spots = []
    for shift in (0, 1):
        where = [jax.random.randint(jax.random.fold_in(stream_key, axis), (), 0, length) for axis, length in enumerate(values.shape)]
        where[longest] = (where[longest] + shift) % values.shape[longest]
        spots.append(tuple(where))
    return values.at[spots[0]].set(least).at[spots[1]].set(largest)


def block_levels(rng, extent, pieces, least, high):
    level, own = 1.0, jax.random.fold_in(rng, 6)
    for position, blocks in pieces:
        steps = jnp.exp(jax.random.uniform(jax.random.fold_in(own, position), (blocks,), jnp.float32, least / len(pieces), high / len(pieces)))
        level = level * jnp.repeat(steps, extent[position] // blocks).reshape([-1 if axis == position else 1 for axis in range(len(extent))])
    return level


def centred(key, shape, scale, reach, cuts=(), kind=jnp.bfloat16):
    values = scale * jax.random.normal(key, shape, jnp.float32)
    if cuts:
        values = values * block_levels(key, shape, cuts, -0.22, 0.18)
    return jnp.clip(values, -reach, reach).astype(kind)


def setup_inputs(seed: int = 0) -> dict:
    arg_keys = jax.random.split(jax.random.key(seed), 11)
    return {
        "ensemble_profiles_before": centred(arg_keys[0], (K, PROFILE_SIZE, COLS), 1.0, 6.0, ((0, 16), (2, 32))),
        "mixing_coefficient": jnp.clip(jnp.exp(math.log(0.24) - 1.5686159 * jax.random.uniform(arg_keys[1], (COLS,), jnp.float32) ** block_levels(arg_keys[1], (COLS,), ((0, 32),), -0.2, 0.2)), 0.05, 0.24),
        "surface_driver": centred(arg_keys[2], (K, COLS), 0.5, 3.0, ((0, 16), (1, 32)), jnp.float32),
        "terrain_indicator": set_ends((jax.random.randint(arg_keys[3], (COLS,), 0, 4) < 3).astype(jnp.int32), jax.random.fold_in(arg_keys[3], 1), 0, 1),
        "measured_profile_position": set_ends(jax.random.randint(arg_keys[4], (N_TILE * OBS_T,), 0, C_TILE), jax.random.fold_in(arg_keys[4], 1), 0, C_TILE - 1).astype(jnp.int32),
        "measured_field_index": set_ends(jax.random.randint(arg_keys[5], (N_TILE * OBS_T,), 0, PROFILE_SIZE), jax.random.fold_in(arg_keys[5], 1), 0, PROFILE_SIZE - 1).astype(jnp.int32),
        "obs_valid": set_ends((jax.random.randint(arg_keys[6], (N_TILE * OBS_T,), 0, 8) < 7).astype(jnp.int32), jax.random.fold_in(arg_keys[6], 1), 0, 1),
        "obs_value": centred(arg_keys[7], (N_TILE * OBS_T,), 1.0, 6.0, ((0, 32),)),
        "obs_error": jnp.clip(jnp.exp(math.log(4.0) - 2.0794415 * jax.random.uniform(arg_keys[8], (N_TILE * OBS_T,), jnp.float32) ** block_levels(arg_keys[8], (N_TILE * OBS_T,), ((0, 32),), -0.2, 0.2)), 0.5, 4.0).astype(jnp.bfloat16),
        "local_weight": jnp.clip(jnp.exp(math.log(0.03) - 3.4011973 * jax.random.uniform(arg_keys[9], (NB_TILE, N_TILE, P_OBS), jnp.float32) ** block_levels(arg_keys[9], (NB_TILE, N_TILE, P_OBS), ((0, 16), (1, 32)), -0.2, 0.2)), 0.001, 0.03),
    }


EXACT = lax.Precision.HIGHEST

def vertical_mixing_step(ensemble_profiles_before, mixing_coefficient, surface_driver, terrain_indicator):
    values = ensemble_profiles_before.astype(jnp.float32)
    above_layer = jnp.concatenate([values[:, :1], values[:, :-1]], axis=1)
    below_layer = jnp.concatenate([values[:, 1:], values[:, -1:]], axis=1)
    diffused = values + mixing_coefficient[None, None, :] * (above_layer - 2.0 * values + below_layer)
    stepped = diffused - 0.05 * values * values * values
    surface = jnp.concatenate([stepped[:, :1] + surface_driver[:, None, :], stepped[:, 1:]], axis=1)
    result = jnp.where(terrain_indicator[None, None, :] > 0, surface, values)
    return result.astype(jnp.bfloat16)

def measurement_operator(background_ensemble, measured_profile_position, measured_field_index):
    profile_sequence = background_ensemble.shape[2]
    unrolled_ensemble = background_ensemble.reshape(background_ensemble.shape[0], -1)
    slot_index = measured_field_index.astype(jnp.int32) * profile_sequence + measured_profile_position.astype(jnp.int32)
    return jnp.take(unrolled_ensemble, slot_index, axis=1)

def prepare(window):
    ensemble_profiles = window.shape[0] - 3
    measured_quantities = window[:ensemble_profiles].astype(jnp.float32)
    average = lax.optimization_barrier(jnp.mean(measured_quantities, axis=0))
    deviation = measured_quantities - average
    innovation = window[ensemble_profiles].astype(jnp.float32) - average
    obs_precision = window[ensemble_profiles + 2].astype(jnp.float32) / window[ensemble_profiles + 1].astype(jnp.float32)
    return (deviation, innovation, obs_precision)

def weights_for(deviation, innovation, precision, portions):
    ensemble_profiles = deviation.shape[0]
    portion_width = deviation.shape[1] // portions
    spread = jnp.zeros((ensemble_profiles, ensemble_profiles), jnp.float32)
    for portion_index in range(portions):
        portion = deviation[:, portion_index * portion_width:(portion_index + 1) * portion_width]
        scaled = portion * precision[None, portion_index * portion_width:(portion_index + 1) * portion_width]
        spread = spread + jnp.dot(scaled, portion.T, precision=EXACT, preferred_element_type=jnp.float32)
    spread = spread / (ensemble_profiles - 1.0)
    pulled = jnp.dot(deviation, precision * innovation, precision=EXACT, preferred_element_type=jnp.float32) / (ensemble_profiles - 1.0)
    identity = jnp.eye(ensemble_profiles, dtype=jnp.float32)
    system = identity + spread
    norm_scale = jnp.sqrt(jnp.sum(system * system))

    def newton(sweep, carry):
        current, inv_root = carry
        middle = 1.5 * identity - 0.5 * jnp.dot(inv_root, current, precision=EXACT)
        return (jnp.dot(current, middle, precision=EXACT), jnp.dot(middle, inv_root, precision=EXACT))
    current, inv_root = lax.fori_loop(0, NS_ITERS, newton, (system / norm_scale, identity))
    inv_root = inv_root / jnp.sqrt(norm_scale)
    inverse = jnp.dot(inv_root, inv_root, precision=EXACT)
    mean_weight = jnp.dot(inverse, pulled, precision=EXACT)
    return inv_root + mean_weight[:, None]

def update(states, transform, land_block):
    values = states.astype(jnp.float32)
    average = lax.optimization_barrier(jnp.mean(values, axis=0))
    deviation = values - average[None]
    moved = jnp.einsum('isc,ij->jsc', deviation, transform, precision=EXACT)
    result = jnp.where(land_block[None, None, :] > 0, average[None] + moved, values)
    return result.astype(jnp.bfloat16)

def reference(ensemble_profiles_before, mixing_coefficient, surface_driver, terrain_indicator, measured_profile_position, measured_field_index, obs_valid, obs_value, obs_error, local_weight):
    background_ensemble = vertical_mixing_step(ensemble_profiles_before, mixing_coefficient, surface_driver, terrain_indicator)
    number_sections = N_TILE
    ensemble_profiles = ensemble_profiles_before.shape[0]
    section_breadth = ensemble_profiles_before.shape[2] // number_sections
    blocks_tile = section_breadth // BLK
    sectioned_ensemble = background_ensemble.reshape(ensemble_profiles, PROFILE_SIZE, number_sections, section_breadth).transpose(2, 0, 1, 3)
    measured_quantities = jax.vmap(measurement_operator)(sectioned_ensemble, measured_profile_position.reshape(number_sections, OBS_T), measured_field_index.reshape(number_sections, OBS_T))
    metadata = jnp.stack([obs_value.reshape(number_sections, OBS_T), obs_error.reshape(number_sections, OBS_T), obs_valid.reshape(number_sections, OBS_T).astype(jnp.bfloat16)], axis=1)
    obs_rows = jnp.concatenate([measured_quantities, metadata], axis=1)
    offsets = jnp.arange(-REACH, REACH + 1, dtype=jnp.int32)
    land_tiles = terrain_indicator.reshape(number_sections, blocks_tile, BLK)

    def one_tile(tile_index):
        chosen = (tile_index + offsets) % number_sections
        window = jnp.take(obs_rows, chosen, axis=0).transpose(1, 0, 2).reshape(ensemble_profiles + 3, -1)
        deviation, innovation, obs_precision = prepare(window)
        tile_states = lax.dynamic_index_in_dim(sectioned_ensemble, tile_index, 0, keepdims=False)
        tile_states = tile_states.reshape(ensemble_profiles, PROFILE_SIZE, blocks_tile, BLK).transpose(2, 0, 1, 3)
        tile_land = lax.dynamic_index_in_dim(land_tiles, tile_index, 0, keepdims=False)
        tile_weight = lax.dynamic_index_in_dim(local_weight, tile_index, 1, keepdims=False)

        def one_block(inputs):
            states, land_block, weight = inputs
            transform = weights_for(deviation, innovation, obs_precision * weight, 2 * REACH + 1)
            return update(states, transform, land_block)
        finished = lax.map(one_block, (tile_states, tile_land, tile_weight))
        return finished.transpose(1, 2, 0, 3).reshape(ensemble_profiles, PROFILE_SIZE, section_breadth)
    analysed = lax.map(one_tile, jnp.arange(number_sections, dtype=jnp.int32))
    return analysed.transpose(1, 2, 0, 3).reshape(ensemble_profiles, PROFILE_SIZE, number_sections * section_breadth)
```

```python
import jax
import jax.numpy as jnp
from jax import lax
from jax.experimental import pallas as pl
from jax.experimental.pallas import tpu as pltpu
from jax.sharding import PartitionSpec as P

REACH = 2
NS_ITERS = 3

F32 = jnp.float32
BF16 = jnp.bfloat16
EXACT = lax.Precision.HIGHEST
VMEM_LIMIT = 40 * 1024 * 1024

MEM = 16
OWN = 4
LAYERS = 40
LANE = 128
ROWS = OWN * LAYERS
MEMBERS = MEM * OWN
PARTS = 4
PART_COLS = 2048 // PARTS
HALF = 16
GROUP = 4
PACK = 40


def call(kernel, out_shape, scratch, flops, nbytes, *args):
    vmem = pl.BlockSpec(memory_space=pltpu.VMEM)
    return pl.pallas_call(
        kernel,
        out_shape=out_shape,
        in_specs=[vmem] * len(args),
        out_specs=jax.tree.map(lambda _: vmem, out_shape),
        scratch_shapes=scratch,
        compiler_params=pltpu.CompilerParams(vmem_limit_bytes=VMEM_LIMIT),
        cost_estimate=pl.CostEstimate(flops=flops, bytes_accessed=nbytes, transcendentals=0),
    )(*args)


def forecast_kernel(
    x_ref, mix_ref, drive_ref, land_ref, pos_ref, field_ref, states_ref, seen_ref, table, seen
):
    layer = lax.broadcasted_iota(jnp.int32, (LAYERS, LANE), 0)
    for block in range(MEM):
        lanes = slice(block * LANE, (block + 1) * LANE)
        mix = mix_ref[block : block + 1, :]
        land = jnp.broadcast_to(land_ref[block : block + 1, :], (LAYERS, LANE)) > 0
        members = []
        for k in range(OWN):
            x = x_ref[k, :, lanes].astype(F32)
            above = jnp.where(layer == 0, x, pltpu.roll(x, 1, 0))
            below = jnp.where(layer == LAYERS - 1, x, pltpu.roll(x, LAYERS - 1, 0))
            stepped = x + mix * (above - 2.0 * x + below) - 0.05 * x * x * x
            stepped = jnp.where(layer == 0, stepped + drive_ref[k : k + 1, lanes], stepped)
            members.append(jnp.where(land, stepped, x))
        result = jnp.concatenate(members, axis=0).astype(BF16)
        states_ref[block] = result
        part, place = divmod(block, MEM // PARTS)
        table[part * ROWS : (part + 1) * ROWS, place * LANE : (place + 1) * LANE] = result

    column = lax.broadcasted_iota(jnp.int32, (PART_COLS, LANE), 0)
    for pair in range(HALF):
        hot, codes = [], []
        for row in (2 * pair, 2 * pair + 1):
            pos = pos_ref[row : row + 1, :]
            hot.append(jnp.where(column == (pos & (PART_COLS - 1)), 1.0, 0.0).astype(BF16))
            codes.append((pos // PART_COLS) * LAYERS + field_ref[row : row + 1, :])
        found = jnp.dot(table[...], jnp.concatenate(hot, axis=1), preferred_element_type=F32)
        for i in range(2):
            half, place = divmod(2 * pair + i, HALF)
            hits = [layer == codes[i] - part * LAYERS for part in range(PARTS)]
            for k in range(OWN):
                total = jnp.zeros((LAYERS, LANE), F32)
                for part in range(PARTS):
                    first = part * ROWS + k * LAYERS
                    total = jnp.where(
                        hits[part],
                        found[first : first + LAYERS, i * LANE : (i + 1) * LANE],
                        total,
                    )
                at = half * OWN * HALF + k * HALF + place
                seen[at : at + 1, :] = jnp.sum(total, axis=0, keepdims=True)
    for half in range(2):
        values = seen[half * OWN * HALF : (half + 1) * OWN * HALF, :].astype(BF16)
        for chip in range(MEM // 2):
            seen_ref[2 * chip + half] = values


def group_places():
    tile = lax.axis_index("tile")
    return tile % GROUP, (tile + GROUP // 2) % GROUP


def sums_kernel(
    seen_ref, w1_ref, w2_ref, value_ref, error_ref, valid_ref, p1_ref, p2_ref, wide, dev_s, inn_s, scaled
):
    core = lax.axis_index("mem") % 2
    _, place2 = group_places()
    across = jnp.where(place2 < 2, 4, 0)
    wide[...] = seen_ref[...].reshape(MEM * OWN * HALF, LANE).astype(F32)
    start = pl.multiple_of(core * HALF, HALF)
    obs_value = value_ref[pl.ds(start, HALF), :].astype(F32)
    base = valid_ref[pl.ds(start, HALF), :].astype(F32) / error_ref[pl.ds(start, HALF), :].astype(F32)
    first_row = lax.broadcasted_iota(jnp.int32, (16, LANE), 0) == 0
    for row in range(HALF):
        lanes = slice(row * LANE, (row + 1) * LANE)
        values = wide[pl.ds(row, MEMBERS, stride=HALF), :]
        mean = jnp.sum(values, axis=0, keepdims=True) * (1.0 / MEMBERS)
        deviation = values - mean
        rounded = deviation.astype(BF16)
        dev_s[0:MEMBERS, lanes] = rounded
        dev_s[MEMBERS : 2 * MEMBERS, lanes] = rounded
        innovation = obs_value[row : row + 1, :] - mean
        inn_s[:, lanes] = jnp.where(first_row, innovation, 0.0).astype(BF16)
        for j in range(12):
            weight = w1_ref[j, row : row + 1, :] if j < 8 else w2_ref[across + (j - 8), row : row + 1, :]
            rinv = base[row : row + 1, :] * weight
            scaled[j * MEMBERS : (j + 1) * MEMBERS, lanes] = (deviation * rinv).astype(BF16)
    last = (((1,), (1,)), ((), ()))
    spread = lax.dot_general(scaled[...], dev_s[...], last, preferred_element_type=F32)
    pulled = lax.dot_general(inn_s[...], scaled[...], last, preferred_element_type=F32)
    left = lax.broadcasted_iota(jnp.int32, (32, LANE), 1) < MEMBERS
    p2_ref[...] = jnp.zeros_like(p2_ref)
    for j in range(12):
        top = spread[j * MEMBERS : j * MEMBERS + 32, :]
        bottom = spread[j * MEMBERS + 32 : (j + 1) * MEMBERS, :]
        packed = jnp.where(left, top, bottom)
        pull = pulled[0:8, (j // 2) * LANE : (j // 2 + 1) * LANE]
        if j < 8:
            p1_ref[j, 0:32, :] = packed
            p1_ref[j, 32:40, :] = pull
        else:
            p2_ref[across + (j - 8), 0:32, :] = packed
            p2_ref[across + (j - 8), 32:40, :] = pull


def regroup_kernel(states_ref, out_ref, wide):
    wide[...] = states_ref[...].reshape(MEM * ROWS, LANE).astype(F32)
    for layer in range(LAYERS):
        out_ref[:, layer * LANE : (layer + 1) * LANE] = wide[
            pl.ds(layer, MEMBERS, stride=LAYERS), :
        ].astype(BF16)


def exact_dot(a, b):
    return jnp.dot(a, b, precision=EXACT, preferred_element_type=F32)


def update_kernel(p1_ref, p2_ref, states_ref, land_ref, out_ref, wide):
    block = lax.axis_index("mem")
    core = block % 2
    place1, place2 = group_places()
    total = jnp.zeros((PACK, LANE), F32)
    for j in range(2 * GROUP):
        q = j // 2
        near = jnp.abs(q - place1) <= REACH
        total = total + jnp.where(near, p1_ref[j], 0.0)
    for j in range(2 * GROUP):
        q = j // 2
        other = (place2 >= 2) if q < 2 else (place2 < 2)
        near = jnp.logical_and(other, jnp.abs(q - place2) <= REACH)
        total = total + jnp.where(near, p2_ref[j], 0.0)
    total = total * (1.0 / (MEMBERS - 1.0))
    upper = total[0:32, :]
    spread = jnp.concatenate([upper, pltpu.roll(upper, MEMBERS, 1)], axis=0)[:, :MEMBERS]
    pull = total[32:40, :]
    pull = jnp.where(core == 0, pull, pltpu.roll(pull, MEMBERS, 1))[:, :MEMBERS]

    rows = lax.broadcasted_iota(jnp.int32, (MEMBERS, MEMBERS), 0)
    cols = lax.broadcasted_iota(jnp.int32, (MEMBERS, MEMBERS), 1)
    identity = jnp.where(rows == cols, 1.0, 0.0)
    system = identity + spread
    square = jnp.sum(jnp.sum(system * system, axis=1, keepdims=True), axis=0, keepdims=True)
    inv_scale = lax.rsqrt(square)
    current = system * inv_scale
    root = 1.5 * identity - 0.5 * current
    current = exact_dot(current, root)
    for sweep in range(1, NS_ITERS):
        middle = 1.5 * identity - 0.5 * exact_dot(root, current)
        if sweep < NS_ITERS - 1:
            current = exact_dot(current, middle)
        root = exact_dot(middle, root)
    inv_root = root * jnp.sqrt(inv_scale)
    mean_weight = exact_dot(exact_dot(pull, inv_root), inv_root)[0:1, :]
    turned = inv_root + mean_weight
    turned = turned + (1.0 - jnp.sum(turned, axis=1, keepdims=True)) * (1.0 / MEMBERS)
    high = turned.astype(BF16)
    low = (turned - high.astype(F32)).astype(BF16)
    both = jnp.concatenate([high, low], axis=0)
    land = jnp.broadcast_to(land_ref[pl.ds(block, 1), :], (MEMBERS, LANE)) > 0
    moved = jnp.dot(both, states_ref[...], preferred_element_type=F32)
    for layer in range(LAYERS):
        lanes = slice(layer * LANE, (layer + 1) * LANE)
        result = jnp.where(
            land,
            moved[:MEMBERS, lanes] + moved[MEMBERS:, lanes],
            states_ref[:, lanes].astype(F32),
        )
        wide[pl.ds(layer, MEMBERS, stride=LAYERS), :] = result
    out_ref[...] = wide[...].astype(BF16).reshape(MEM, ROWS, LANE)


def shape(*dims, dtype=BF16):
    return jax.ShapeDtypeStruct(dims, dtype)


def exchange_groups(tiles, first):
    return [
        [
            (2 * chip + core) * tiles + (start + q) % tiles
            for q in range(GROUP)
            for core in range(2)
        ]
        for chip in range(MEM // 2)
        for start in range(first, tiles + first, GROUP)
    ]


def group_exchange(parts, groups):
    return lax.all_to_all(parts, ("mem", "tile"), 0, 0, axis_index_groups=groups, tiled=True)


def on_device(
    ensemble_profiles_before,
    mixing_coefficient,
    surface_driver,
    terrain_indicator,
    measured_profile_position,
    measured_field_index,
    obs_valid,
    obs_value,
    obs_error,
    local_weight,
):
    tiles = lax.axis_size("tile")
    groups1, groups2 = exchange_groups(tiles, 0), exchange_groups(tiles, GROUP // 2)
    place1, place2 = group_places()
    land = terrain_indicator.reshape(MEM, LANE)

    slabs = local_weight.reshape(2 * REACH + 1, 2 * HALF, LANE)
    slabs = jnp.pad(slabs, ((1, 1), (0, 0), (0, 0)))
    for_group1 = lax.dynamic_slice_in_dim(slabs, 3 - place1, GROUP).reshape(2 * GROUP, HALF, LANE)
    for_group2 = lax.dynamic_slice_in_dim(slabs, 3 - place2, GROUP).reshape(2 * GROUP, HALF, LANE)

    states, seen = call(
        forecast_kernel,
        (shape(MEM, ROWS, LANE), shape(MEM, OWN * HALF, LANE)),
        [pltpu.VMEM((PARTS * ROWS, PART_COLS), BF16), pltpu.VMEM((2 * OWN * HALF, LANE), F32)],
        2 * 4096 * ROWS * 2048,
        2000000,
        ensemble_profiles_before,
        mixing_coefficient.reshape(MEM, LANE),
        surface_driver,
        land,
        measured_profile_position.reshape(2 * HALF, LANE),
        measured_field_index.reshape(2 * HALF, LANE),
    )
    seen = lax.all_to_all(seen, "mem", 0, 0, tiled=True)
    weights1 = group_exchange(for_group1, groups1)
    weights2 = group_exchange(for_group2, groups2)
    states = lax.all_to_all(states, "mem", 0, 0, tiled=True)

    sums1, sums2 = call(
        sums_kernel,
        (shape(2 * GROUP, PACK, LANE, dtype=F32), shape(2 * GROUP, PACK, LANE, dtype=F32)),
        [
            pltpu.VMEM((MEM * OWN * HALF, LANE), F32),
            pltpu.VMEM((2 * MEMBERS, HALF * LANE), BF16),
            pltpu.VMEM((16, HALF * LANE), BF16),
            pltpu.VMEM((12 * MEMBERS, HALF * LANE), BF16),
        ],
        2 * 768 * 128 * 2048,
        1000000,
        seen,
        weights1,
        weights2,
        obs_value.reshape(2 * HALF, LANE),
        obs_error.reshape(2 * HALF, LANE),
        obs_valid.reshape(2 * HALF, LANE),
    )
    sums1 = group_exchange(sums1, groups1)
    sums2 = group_exchange(sums2, groups2)
    states = call(
        regroup_kernel,
        shape(MEMBERS, LAYERS * LANE),
        [pltpu.VMEM((MEM * ROWS, LANE), F32)],
        MEM * ROWS * LANE,
        1300000,
        states,
    )
    analysed = call(
        update_kernel,
        shape(MEM, ROWS, LANE),
        [pltpu.VMEM((MEM * ROWS, LANE), F32)],
        2 * 128 * 64 * 5120,
        1300000,
        sums1,
        sums2,
        states,
        land,
    )
    analysed = lax.all_to_all(analysed, "mem", 0, 0, tiled=True)
    return (
        analysed.reshape(MEM, OWN, LAYERS, LANE)
        .transpose(1, 2, 0, 3)
        .reshape(OWN, LAYERS, MEM * LANE)
    )


def solution(mesh):
    in_specs = (
        P("mem", None, "tile"),
        P("tile"),
        P("mem", "tile"),
        P("tile"),
        P("tile"),
        P("tile"),
        P("tile"),
        P("tile"),
        P("tile"),
        P("mem", "tile", None),
    )
    out_specs = P("mem", None, "tile")
    return jax.shard_map(
        on_device, mesh=mesh, in_specs=in_specs, out_specs=out_specs, check_vma=False
    )
```

```python
import jax
import jax.numpy as jnp
from jax import lax
from jax.experimental import pallas as pl
from jax.experimental.pallas import tpu as pltpu
from jax.sharding import PartitionSpec as P

REACH = 2
NS_ITERS = 3

F32 = jnp.float32
BF16 = jnp.bfloat16
EXACT = lax.Precision.HIGHEST
VMEM_LIMIT = 40 * 1024 * 1024
FORECAST_VMEM = 62 * 1024 * 1024

MEM = 16
OWN = 4
LAYERS = 40
LANE = 128
ROWS = OWN * LAYERS
MEMBERS = MEM * OWN
PARTS = 4
PART_COLS = 2048 // PARTS
SLOT_ROWS = 32
PACK = 40


def call(kernel, out_shape, scratch, flops, nbytes, *args, where=pltpu.VMEM, vmem=VMEM_LIMIT):
    block = pl.BlockSpec(memory_space=pltpu.VMEM)
    return pl.pallas_call(
        kernel,
        out_shape=out_shape,
        in_specs=[pl.BlockSpec(memory_space=where)] * len(args),
        out_specs=jax.tree.map(lambda _: block, out_shape),
        scratch_shapes=scratch,
        compiler_params=pltpu.CompilerParams(vmem_limit_bytes=vmem),
        cost_estimate=pl.CostEstimate(flops=flops, bytes_accessed=nbytes, transcendentals=0),
    )(*args)


def forecast_kernel(*refs):
    sources, (states_ref, seen_ref, table, seen, *buffers, done) = refs[:6], refs[6:]
    copies = [
        pltpu.make_async_copy(source, buffer, done.at[i])
        for i, (source, buffer) in enumerate(zip(sources, buffers))
    ]
    for copy in copies:
        copy.start()
    for copy in copies:
        copy.wait()
    x_ref, mix_ref, drive_ref, land_ref, pos_ref, field_ref = buffers
    layer = lax.broadcasted_iota(jnp.int32, (LAYERS, LANE), 0)
    for block in range(MEM):
        lanes = slice(block * LANE, (block + 1) * LANE)
        mix = mix_ref[block : block + 1, :]
        land = jnp.broadcast_to(land_ref[block : block + 1, :], (LAYERS, LANE)) > 0
        members = []
        for k in range(OWN):
            x = x_ref[k, :, lanes].astype(F32)
            above = jnp.where(layer == 0, x, pltpu.roll(x, 1, 0))
            below = jnp.where(layer == LAYERS - 1, x, pltpu.roll(x, LAYERS - 1, 0))
            stepped = x + mix * (above - 2.0 * x + below) - 0.05 * x * x * x
            stepped = jnp.where(layer == 0, stepped + drive_ref[k : k + 1, lanes], stepped)
            members.append(jnp.where(land, stepped, x))
        result = jnp.concatenate(members, axis=0).astype(BF16)
        states_ref[block] = result
        part, place = divmod(block, MEM // PARTS)
        table[part * ROWS : (part + 1) * ROWS, place * LANE : (place + 1) * LANE] = result

    column = lax.broadcasted_iota(jnp.int32, (PART_COLS, LANE), 0)
    for pair in range(SLOT_ROWS // 2):
        hot, codes = [], []
        for row in (2 * pair, 2 * pair + 1):
            pos = pos_ref[row : row + 1, :]
            hot.append(jnp.where(column == (pos & (PART_COLS - 1)), 1.0, 0.0).astype(BF16))
            codes.append((pos // PART_COLS) * LAYERS + field_ref[row : row + 1, :])
        found = jnp.dot(table[...], jnp.concatenate(hot, axis=1), preferred_element_type=F32)
        for i in range(2):
            hits = [layer == codes[i] - part * LAYERS for part in range(PARTS)]
            for k in range(OWN):
                total = jnp.zeros((LAYERS, LANE), F32)
                for part in range(PARTS):
                    first = part * ROWS + k * LAYERS
                    total = jnp.where(
                        hits[part],
                        found[first : first + LAYERS, i * LANE : (i + 1) * LANE],
                        total,
                    )
                at = k * SLOT_ROWS + 2 * pair + i
                seen[at : at + 1, :] = jnp.sum(total, axis=0, keepdims=True)
    values = seen[...].astype(BF16)
    for device in range(MEM):
        seen_ref[device] = values


def sums_kernel(
    seen_ref, own_ref, near_ref, far_ref, value_ref, error_ref, valid_ref,
    own_sum, near_sum, far_sum, wide, dev_s, inn_s, scaled,
):
    weights = (own_ref, near_ref.at[0], near_ref.at[1], far_ref.at[0], far_ref.at[1])
    wide[...] = seen_ref[...].reshape(MEMBERS * SLOT_ROWS, LANE).astype(F32)
    obs_value = value_ref[...].astype(F32)
    base = valid_ref[...].astype(F32) / error_ref[...].astype(F32)
    first_row = lax.broadcasted_iota(jnp.int32, (16, LANE), 0) == 0
    for row in range(SLOT_ROWS):
        lanes = slice(row * LANE, (row + 1) * LANE)
        values = wide[pl.ds(row, MEMBERS, stride=SLOT_ROWS), :]
        mean = jnp.sum(values, axis=0, keepdims=True) * (1.0 / MEMBERS)
        deviation = values - mean
        rounded = deviation.astype(BF16)
        dev_s[0:MEMBERS, lanes] = rounded
        dev_s[MEMBERS : 2 * MEMBERS, lanes] = rounded
        innovation = obs_value[row : row + 1, :] - mean
        inn_s[:, lanes] = jnp.where(first_row, innovation, 0.0).astype(BF16)
        for j in range(5):
            rinv = base[row : row + 1, :] * weights[j][row : row + 1, :]
            scaled[j * MEMBERS : (j + 1) * MEMBERS, lanes] = (deviation * rinv).astype(BF16)
    last = (((1,), (1,)), ((), ()))
    spread = lax.dot_general(scaled[...], dev_s[...], last, preferred_element_type=F32)
    pulled = lax.dot_general(inn_s[...], scaled[...], last, preferred_element_type=F32)
    left = lax.broadcasted_iota(jnp.int32, (32, LANE), 1) < MEMBERS
    outs = (own_sum, near_sum.at[0], near_sum.at[1], far_sum.at[0], far_sum.at[1])
    for j, out in enumerate(outs):
        top = spread[j * MEMBERS : j * MEMBERS + 32, :]
        bottom = spread[j * MEMBERS + 32 : (j + 1) * MEMBERS, :]
        out[0:32, :] = jnp.where(left, top, bottom)
        pull = pulled[0:8, j * MEMBERS : (j + 1) * MEMBERS]
        out[32:40, :] = jnp.concatenate([pull, pull], axis=1)


def regroup_kernel(states_ref, out_ref, wide):
    wide[...] = states_ref[...].reshape(MEM * ROWS, LANE).astype(F32)
    for layer in range(LAYERS):
        out_ref[:, layer * LANE : (layer + 1) * LANE] = wide[
            pl.ds(layer, MEMBERS, stride=LAYERS), :
        ].astype(BF16)


def exact_dot(a, b):
    return jnp.dot(a, b, precision=EXACT, preferred_element_type=F32)


def update_kernel(own_ref, near_ref, far_ref, rest_ref, states_ref, land_ref, out_ref, wide):
    block = lax.axis_index("mem")
    total = own_ref[...] + near_ref[0] + far_ref[0] + rest_ref[...]
    total = total * (1.0 / (MEMBERS - 1.0))
    upper = total[0:32, :]
    spread = jnp.concatenate([upper, pltpu.roll(upper, MEMBERS, 1)], axis=0)[:, :MEMBERS]
    pull = total[32:40, :MEMBERS]

    rows = lax.broadcasted_iota(jnp.int32, (MEMBERS, MEMBERS), 0)
    cols = lax.broadcasted_iota(jnp.int32, (MEMBERS, MEMBERS), 1)
    identity = jnp.where(rows == cols, 1.0, 0.0)
    system = identity + spread
    square = jnp.sum(jnp.sum(system * system, axis=1, keepdims=True), axis=0, keepdims=True)
    inv_scale = lax.rsqrt(square)
    current = system * inv_scale
    root = 1.5 * identity - 0.5 * current
    current = exact_dot(current, root)
    for sweep in range(1, NS_ITERS):
        middle = 1.5 * identity - 0.5 * exact_dot(root, current)
        if sweep < NS_ITERS - 1:
            current = exact_dot(current, middle)
        root = exact_dot(middle, root)
    inv_root = root * jnp.sqrt(inv_scale)
    mean_weight = exact_dot(exact_dot(pull, inv_root), inv_root)[0:1, :]
    turned = inv_root + mean_weight
    turned = turned + (1.0 - jnp.sum(turned, axis=1, keepdims=True)) * (1.0 / MEMBERS)
    high = turned.astype(BF16)
    low = (turned - high.astype(F32)).astype(BF16)
    both = jnp.concatenate([high, low], axis=0)
    land = jnp.broadcast_to(land_ref[pl.ds(block, 1), :], (MEMBERS, LANE)) > 0
    moved = jnp.dot(both, states_ref[...], preferred_element_type=F32)
    for layer in range(LAYERS):
        lanes = slice(layer * LANE, (layer + 1) * LANE)
        result = jnp.where(
            land,
            moved[:MEMBERS, lanes] + moved[MEMBERS:, lanes],
            states_ref[:, lanes].astype(F32),
        )
        wide[pl.ds(layer, MEMBERS, stride=LAYERS), :] = result
    out_ref[...] = wide[...].astype(BF16).reshape(MEM, ROWS, LANE)


def shape(*dims, dtype=BF16):
    return jax.ShapeDtypeStruct(dims, dtype)


def to_tile(value, steps):
    mem, tiles = lax.axis_size("mem"), lax.axis_size("tile")
    pairs = [
        (m * tiles + t, m * tiles + (t + (steps if m % 2 else -steps)) % tiles)
        for m in range(mem)
        for t in range(tiles)
    ]
    return lax.ppermute(value, ("mem", "tile"), pairs)


def to_other_core(value):
    return lax.ppermute(value, "mem", [(m, m ^ 1) for m in range(lax.axis_size("mem"))])


def on_device(
    ensemble_profiles_before,
    mixing_coefficient,
    surface_driver,
    terrain_indicator,
    measured_profile_position,
    measured_field_index,
    obs_valid,
    obs_value,
    obs_error,
    local_weight,
):
    land = terrain_indicator.reshape(MEM, LANE)
    slabs = local_weight.reshape(2 * REACH + 1, SLOT_ROWS, LANE)

    inputs = (
        ensemble_profiles_before,
        mixing_coefficient.reshape(MEM, LANE),
        surface_driver,
        land,
        measured_profile_position.reshape(SLOT_ROWS, LANE),
        measured_field_index.reshape(SLOT_ROWS, LANE),
    )
    states, seen = call(
        forecast_kernel,
        (shape(MEM, ROWS, LANE), shape(MEM, OWN * SLOT_ROWS, LANE)),
        [pltpu.VMEM((PARTS * ROWS, PART_COLS), BF16), pltpu.VMEM((OWN * SLOT_ROWS, LANE), F32)]
        + [pltpu.VMEM(array.shape, array.dtype) for array in inputs]
        + [pltpu.SemaphoreType.DMA((len(inputs),))],
        2 * 4096 * ROWS * 2048,
        2000000,
        *inputs,
        where=pl.ANY,
        vmem=FORECAST_VMEM,
    )
    slabs, seen = lax.optimization_barrier((slabs, seen))
    ahead = lax.axis_index("mem") % 2 == 1
    lower, upper = slabs[REACH - 1 :: -1][:REACH], slabs[REACH + 1 :]
    kept, given = jnp.where(ahead, lower, upper), jnp.where(ahead, upper, lower)
    taken = to_other_core(given)
    weights = [
        to_tile(jnp.stack([kept[d - 1], taken[d - 1]]), -d) for d in range(1, REACH + 1)
    ]
    seen = lax.all_to_all(seen, "mem", 0, 0, tiled=True)
    states, seen, weights = lax.optimization_barrier((states, seen, weights))
    states = lax.all_to_all(states, "mem", 0, 0, tiled=True)

    sums = call(
        sums_kernel,
        (shape(PACK, LANE, dtype=F32),) + (shape(2, PACK, LANE, dtype=F32),) * REACH,
        [
            pltpu.VMEM((MEMBERS * SLOT_ROWS, LANE), F32),
            pltpu.VMEM((2 * MEMBERS, SLOT_ROWS * LANE), BF16),
            pltpu.VMEM((16, SLOT_ROWS * LANE), BF16),
            pltpu.VMEM((5 * MEMBERS, SLOT_ROWS * LANE), BF16),
        ],
        2 * 768 * 128 * 2048,
        1000000,
        seen,
        slabs[REACH],
        *weights,
        obs_value.reshape(SLOT_ROWS, LANE),
        obs_error.reshape(SLOT_ROWS, LANE),
        obs_valid.reshape(SLOT_ROWS, LANE),
    )
    own = sums[0]
    near, far = [to_tile(part, d) for d, part in enumerate(sums[1:], 1)]
    rest = to_other_core(near[1] + far[1])
    states = call(
        regroup_kernel,
        shape(MEMBERS, LAYERS * LANE),
        [pltpu.VMEM((MEM * ROWS, LANE), F32)],
        MEM * ROWS * LANE,
        1300000,
        states,
    )
    analysed = call(
        update_kernel,
        shape(MEM, ROWS, LANE),
        [pltpu.VMEM((MEM * ROWS, LANE), F32)],
        2 * 128 * 64 * 5120,
        1300000,
        own,
        near,
        far,
        rest,
        states,
        land,
    )
    analysed = lax.all_to_all(analysed, "mem", 0, 0, tiled=True)
    return (
        analysed.reshape(MEM, OWN, LAYERS, LANE)
        .transpose(1, 2, 0, 3)
        .reshape(OWN, LAYERS, MEM * LANE)
    )


def solution(mesh):
    in_specs = (
        P("mem", None, "tile"),
        P("tile"),
        P("mem", "tile"),
        P("tile"),
        P("tile"),
        P("tile"),
        P("tile"),
        P("tile"),
        P("tile"),
        P("mem", "tile", None),
    )
    out_specs = P("mem", None, "tile")
    return jax.shard_map(
        on_device, mesh=mesh, in_specs=in_specs, out_specs=out_specs, check_vma=False
    )
```

```python
import jax
import jax.numpy as jnp
from jax import lax
from jax.experimental import pallas as pl
from jax.experimental.pallas import tpu as pltpu
from jax.sharding import PartitionSpec as P

REACH = 2
NS_ITERS = 3

F32 = jnp.float32
BF16 = jnp.bfloat16
VMEM_LIMIT = 40 * 1024 * 1024
SUMS_FLOPS = 60_000_000_000
FORECAST_VMEM = 62 * 1024 * 1024

MEM = 16
OWN = 4
LAYERS = 40
LANE = 128
ROWS = OWN * LAYERS
MEMBERS = MEM * OWN
PARTS = 4
PART_COLS = 2048 // PARTS
SLOT_ROWS = 32
PACK = 40


def call(kernel, out_shape, scratch, flops, nbytes, *args, where=pltpu.VMEM, vmem=VMEM_LIMIT):
    block = pl.BlockSpec(memory_space=where)
    return pl.pallas_call(
        kernel,
        out_shape=out_shape,
        in_specs=[block] * len(args),
        out_specs=jax.tree.map(lambda _: block, out_shape),
        scratch_shapes=scratch,
        compiler_params=pltpu.CompilerParams(vmem_limit_bytes=vmem),
        cost_estimate=pl.CostEstimate(flops=flops, bytes_accessed=nbytes, transcendentals=0),
    )(*args)


def forecast_kernel(*refs):
    sources, (states_ref, seen_ref, table, seen, states, rounded, *buffers, done, sent) = refs[:6], refs[6:]
    copies = [
        pltpu.make_async_copy(source, buffer, done.at[i])
        for i, (source, buffer) in enumerate(zip(sources, buffers))
    ]
    for copy in copies:
        copy.start()
    for copy in copies:
        copy.wait()
    x_ref, mix_ref, drive_ref, land_ref, pos_ref, field_ref = buffers
    layer = lax.broadcasted_iota(jnp.int32, (LAYERS, LANE), 0)
    for block in range(MEM):
        lanes = slice(block * LANE, (block + 1) * LANE)
        mix = mix_ref[block : block + 1, :]
        land = jnp.broadcast_to(land_ref[block : block + 1, :], (LAYERS, LANE)) > 0
        members = []
        for k in range(OWN):
            x = x_ref[k, :, lanes].astype(F32)
            above = jnp.where(layer == 0, x, pltpu.roll(x, 1, 0))
            below = jnp.where(layer == LAYERS - 1, x, pltpu.roll(x, LAYERS - 1, 0))
            stepped = x + mix * (above - 2.0 * x + below) - 0.05 * x * x * x
            stepped = jnp.where(layer == 0, stepped + drive_ref[k : k + 1, lanes], stepped)
            members.append(jnp.where(land, stepped, x))
        result = jnp.concatenate(members, axis=0).astype(BF16)
        states[block] = result
        part, place = divmod(block, MEM // PARTS)
        table[part * ROWS : (part + 1) * ROWS, place * LANE : (place + 1) * LANE] = result

    out_copies = [pltpu.make_async_copy(states, states_ref, sent.at[MEM])]
    out_copies[0].start()

    column = lax.broadcasted_iota(jnp.int32, (PART_COLS, LANE), 0).astype(jnp.int16)
    for pair in range(SLOT_ROWS // 2):
        hot, codes = [], []
        for row in (2 * pair, 2 * pair + 1):
            pos = pos_ref[row : row + 1, :]
            place = (pos & (PART_COLS - 1)).astype(jnp.int16)
            hot.append(jnp.where(column == place, jnp.ones((), BF16), jnp.zeros((), BF16)))
            codes.append((pos // PART_COLS) * LAYERS + field_ref[row : row + 1, :])
        found = jnp.dot(table[...], jnp.concatenate(hot, axis=1), preferred_element_type=F32)
        for i in range(2):
            hits = [layer == codes[i] - part * LAYERS for part in range(PARTS)]
            for k in range(OWN):
                total = jnp.zeros((LAYERS, LANE), F32)
                for part in range(PARTS):
                    first = part * ROWS + k * LAYERS
                    total = jnp.where(
                        hits[part],
                        found[first : first + LAYERS, i * LANE : (i + 1) * LANE],
                        total,
                    )
                at = k * SLOT_ROWS + 2 * pair + i
                seen[at : at + 1, :] = jnp.sum(total, axis=0, keepdims=True)
    rounded[...] = seen[...].astype(BF16)
    for device in range(MEM):
        copy = pltpu.make_async_copy(rounded, seen_ref.at[device], sent.at[device])
        copy.start()
        out_copies.append(copy)
    for copy in out_copies:
        copy.wait()


def sums_kernel(
    seen_ref, own_ref, near_ref, far_ref, value_ref, base_ref,
    own_sum, near_sum, far_sum, wide, terms, scaled,
):
    weights = (own_ref, near_ref.at[0], near_ref.at[1], far_ref.at[0], far_ref.at[1])
    wide[...] = seen_ref[...].reshape(MEMBERS * SLOT_ROWS, LANE).astype(F32)
    obs_value, base = value_ref[...], base_ref[...]
    first_row = lax.broadcasted_iota(jnp.int32, (16, LANE), 0) == 0
    for row in range(SLOT_ROWS):
        lanes = slice(row * LANE, (row + 1) * LANE)
        values = wide[pl.ds(row, MEMBERS, stride=SLOT_ROWS), :]
        mean = jnp.sum(values, axis=0, keepdims=True) * (1.0 / MEMBERS)
        deviation = values - mean
        terms[0:MEMBERS, lanes] = deviation.astype(BF16)
        innovation = obs_value[row : row + 1, :] - mean
        terms[MEMBERS:, lanes] = jnp.where(first_row, innovation, 0.0).astype(BF16)
        for j in range(5):
            rinv = base[row : row + 1, :] * weights[j][row : row + 1, :]
            scaled[j * MEMBERS : (j + 1) * MEMBERS, lanes] = (deviation * rinv).astype(BF16)
    last = (((1,), (1,)), ((), ()))
    sums = lax.dot_general(terms[...], scaled[...], last, preferred_element_type=F32)
    left = lax.broadcasted_iota(jnp.int32, (32, LANE), 1) < MEMBERS
    outs = (own_sum, near_sum.at[0], near_sum.at[1], far_sum.at[0], far_sum.at[1])
    for j, out in enumerate(outs):
        first = j // 2 * LANE
        part = sums[:, first : min(first + LANE, 5 * MEMBERS)]
        if j == 4:
            part = jnp.concatenate([part, part], axis=1)
        turned = pltpu.roll(part, MEMBERS, 1)
        direct, moved = (part, turned) if j % 2 == 0 else (turned, part)
        out[0:32, :] = jnp.where(left, direct[0:32, :], moved[32:64, :])
        out[32:40, :] = direct[64:72, :]


def regroup_kernel(states_ref, out_ref, wide):
    wide[...] = states_ref[...].reshape(MEM * ROWS, LANE).astype(F32)
    for layer in range(LAYERS):
        out_ref[:, layer * LANE : (layer + 1) * LANE] = wide[
            pl.ds(layer, MEMBERS, stride=LAYERS), :
        ].astype(BF16)


def split(value):
    high = value.astype(BF16)
    return high, (value - high.astype(F32)).astype(BF16)


def split_dot(a, b):
    a_high, a_low = split(a)
    b_high, b_low = split(b)
    left = jnp.concatenate([a_high, a_high, a_low], axis=1)
    right = jnp.concatenate([b_high, b_low, b_high], axis=0)
    return jnp.dot(left, right, preferred_element_type=F32)


def update_kernel(own_ref, near_ref, far_ref, rest_ref, states_ref, land_ref, out_ref, wide):
    block = lax.axis_index("mem")
    total = own_ref[...] + near_ref[0] + far_ref[0] + rest_ref[...]
    total = total * (1.0 / (MEMBERS - 1.0))
    upper = total[0:32, :]
    spread = jnp.concatenate([upper, pltpu.roll(upper, MEMBERS, 1)], axis=0)[:, :MEMBERS]
    pull = total[32:40, :MEMBERS]

    rows = lax.broadcasted_iota(jnp.int32, (MEMBERS, MEMBERS), 0)
    cols = lax.broadcasted_iota(jnp.int32, (MEMBERS, MEMBERS), 1)
    identity = jnp.where(rows == cols, 1.0, 0.0)
    system = identity + spread
    square = jnp.sum(jnp.sum(system * system, axis=1, keepdims=True), axis=0, keepdims=True)
    inv_scale = lax.rsqrt(square)
    current = system * inv_scale
    root = 1.5 * identity - 0.5 * current
    current = split_dot(current, root)
    for sweep in range(1, NS_ITERS):
        middle = 1.5 * identity - 0.5 * split_dot(root, current)
        if sweep < NS_ITERS - 1:
            current = split_dot(current, middle)
        root = split_dot(middle, root)
    inv_root = root * jnp.sqrt(inv_scale)
    mean_weight = split_dot(split_dot(pull, inv_root), inv_root)[0:1, :]
    turned = inv_root + mean_weight
    turned = turned + (1.0 - jnp.sum(turned, axis=1, keepdims=True)) * (1.0 / MEMBERS)
    both = jnp.concatenate(split(turned), axis=0)
    land = jnp.broadcast_to(land_ref[pl.ds(block, 1), :], (MEMBERS, LANE)) > 0
    moved = jnp.dot(both, states_ref[...], preferred_element_type=F32)
    for layer in range(LAYERS):
        lanes = slice(layer * LANE, (layer + 1) * LANE)
        result = jnp.where(
            land,
            moved[:MEMBERS, lanes] + moved[MEMBERS:, lanes],
            states_ref[:, lanes].astype(F32),
        )
        wide[pl.ds(layer, MEMBERS, stride=LAYERS), :] = result
    out_ref[...] = wide[...].astype(BF16).reshape(MEM, ROWS, LANE)


def shape(*dims, dtype=BF16):
    return jax.ShapeDtypeStruct(dims, dtype)


def to_tile(value, steps):
    mem, tiles = lax.axis_size("mem"), lax.axis_size("tile")
    pairs = [
        (m * tiles + t, m * tiles + (t + (steps if m % 2 else -steps)) % tiles)
        for m in range(mem)
        for t in range(tiles)
    ]
    return lax.ppermute(value, ("mem", "tile"), pairs)


def to_other_core(value):
    return lax.ppermute(value, "mem", [(m, m ^ 1) for m in range(lax.axis_size("mem"))])


def on_device(
    ensemble_profiles_before,
    mixing_coefficient,
    surface_driver,
    terrain_indicator,
    measured_profile_position,
    measured_field_index,
    obs_valid,
    obs_value,
    obs_error,
    local_weight,
):
    land = terrain_indicator.reshape(MEM, LANE)
    slabs = local_weight.reshape(2 * REACH + 1, SLOT_ROWS, LANE)

    inputs = (
        ensemble_profiles_before,
        mixing_coefficient.reshape(MEM, LANE),
        surface_driver,
        land,
        measured_profile_position.reshape(SLOT_ROWS, LANE),
        measured_field_index.reshape(SLOT_ROWS, LANE),
    )
    states, seen = call(
        forecast_kernel,
        (shape(MEM, ROWS, LANE), shape(MEM, OWN * SLOT_ROWS, LANE)),
        [pltpu.VMEM((PARTS * ROWS, PART_COLS), BF16), pltpu.VMEM((OWN * SLOT_ROWS, LANE), F32)]
        + [pltpu.VMEM((MEM, ROWS, LANE), BF16), pltpu.VMEM((OWN * SLOT_ROWS, LANE), BF16)]
        + [pltpu.VMEM(array.shape, array.dtype) for array in inputs]
        + [pltpu.SemaphoreType.DMA((len(inputs),)), pltpu.SemaphoreType.DMA((MEM + 1,))],
        2 * 4096 * ROWS * 2048,
        2000000,
        *inputs,
        where=pl.ANY,
        vmem=FORECAST_VMEM,
    )
    slabs, obs_value, obs_error, obs_valid, seen = lax.optimization_barrier(
        (slabs, obs_value, obs_error, obs_valid, seen)
    )
    own_weight = slabs[REACH]
    value = obs_value.astype(F32).reshape(SLOT_ROWS, LANE)
    base = (obs_valid.astype(F32) / obs_error.astype(F32)).reshape(SLOT_ROWS, LANE)
    ahead = lax.axis_index("mem") % 2 == 1
    lower, upper = slabs[REACH - 1 :: -1][:REACH], slabs[REACH + 1 :]
    kept, given = jnp.where(ahead, lower, upper), jnp.where(ahead, upper, lower)
    taken = to_other_core(given)
    weights = [
        to_tile(jnp.stack([kept[d - 1], taken[d - 1]]), -d) for d in range(1, REACH + 1)
    ]
    seen = lax.all_to_all(seen, "mem", 0, 0, tiled=True)
    states, seen, taken, own_weight, value, base = lax.optimization_barrier(
        (states, seen, taken, own_weight, value, base)
    )
    states = lax.all_to_all(states, "mem", 0, 0, tiled=True)

    sums = call(
        sums_kernel,
        (shape(PACK, LANE, dtype=F32),) + (shape(2, PACK, LANE, dtype=F32),) * REACH,
        [
            pltpu.VMEM((MEMBERS * SLOT_ROWS, LANE), F32),
            pltpu.VMEM((MEMBERS + 16, SLOT_ROWS * LANE), BF16),
            pltpu.VMEM((5 * MEMBERS, SLOT_ROWS * LANE), BF16),
        ],
        SUMS_FLOPS,
        1000000,
        seen,
        own_weight,
        *weights,
        value,
        base,
    )
    own = sums[0]
    near, far = [to_tile(part, d) for d, part in enumerate(sums[1:], 1)]
    rest = to_other_core(near[1] + far[1])
    states = call(
        regroup_kernel,
        shape(MEMBERS, LAYERS * LANE),
        [pltpu.VMEM((MEM * ROWS, LANE), F32)],
        MEM * ROWS * LANE,
        1300000,
        states,
    )
    analysed = call(
        update_kernel,
        shape(MEM, ROWS, LANE),
        [pltpu.VMEM((MEM * ROWS, LANE), F32)],
        2 * 128 * 64 * 5120,
        1300000,
        own,
        near,
        far,
        rest,
        states,
        land,
    )
    analysed = lax.all_to_all(analysed, "mem", 0, 0, tiled=True)
    return (
        analysed.reshape(MEM, OWN, LAYERS, LANE)
        .transpose(1, 2, 0, 3)
        .reshape(OWN, LAYERS, MEM * LANE)
    )


def solution(mesh):
    in_specs = (
        P("mem", None, "tile"),
        P("tile"),
        P("mem", "tile"),
        P("tile"),
        P("tile"),
        P("tile"),
        P("tile"),
        P("tile"),
        P("tile"),
        P("mem", "tile", None),
    )
    out_specs = P("mem", None, "tile")
    return jax.shard_map(
        on_device, mesh=mesh, in_specs=in_specs, out_specs=out_specs, check_vma=False
    )
```

```python
import jax
import jax.numpy as jnp
from jax import lax
from jax.experimental import pallas as pl
from jax.experimental.pallas import tpu as pltpu
from jax.sharding import PartitionSpec as P

REACH = 2
NS_ITERS = 3

F32 = jnp.float32
BF16 = jnp.bfloat16
VMEM_LIMIT = 40 * 1024 * 1024
SUMS_FLOPS = 60_000_000_000
FORECAST_VMEM = 62 * 1024 * 1024

MEM = 16
OWN = 4
LAYERS = 40
LANE = 128
ROWS = OWN * LAYERS
MEMBERS = MEM * OWN
PARTS = 4
PART_COLS = 2048 // PARTS
SLOT_ROWS = 32
PACK = 40


def call(kernel, out_shape, scratch, flops, nbytes, *args, where=pltpu.VMEM, vmem=VMEM_LIMIT):
    block = pl.BlockSpec(memory_space=where)
    return pl.pallas_call(
        kernel,
        out_shape=out_shape,
        in_specs=[block] * len(args),
        out_specs=jax.tree.map(lambda _: block, out_shape),
        scratch_shapes=scratch,
        compiler_params=pltpu.CompilerParams(vmem_limit_bytes=vmem),
        cost_estimate=pl.CostEstimate(flops=flops, bytes_accessed=nbytes, transcendentals=0),
    )(*args)


def forecast_kernel(*refs):
    sources, (states_ref, seen_ref, table, seen, states, rounded, *buffers, done, sent) = refs[:6], refs[6:]
    copies = [
        pltpu.make_async_copy(source, buffer, done.at[i])
        for i, (source, buffer) in enumerate(zip(sources, buffers))
    ]
    for copy in copies:
        copy.start()
    for copy in copies:
        copy.wait()
    x_ref, mix_ref, drive_ref, land_ref, pos_ref, field_ref = buffers
    layer = lax.broadcasted_iota(jnp.int32, (LAYERS, LANE), 0)
    for block in range(MEM):
        lanes = slice(block * LANE, (block + 1) * LANE)
        mix = mix_ref[block : block + 1, :]
        land = jnp.broadcast_to(land_ref[block : block + 1, :], (LAYERS, LANE)) > 0
        members = []
        for k in range(OWN):
            x = x_ref[k, :, lanes].astype(F32)
            above = jnp.where(layer == 0, x, pltpu.roll(x, 1, 0))
            below = jnp.where(layer == LAYERS - 1, x, pltpu.roll(x, LAYERS - 1, 0))
            stepped = x + mix * (above - 2.0 * x + below) - 0.05 * x * x * x
            stepped = jnp.where(layer == 0, stepped + drive_ref[k : k + 1, lanes], stepped)
            members.append(jnp.where(land, stepped, x))
        result = jnp.concatenate(members, axis=0).astype(BF16)
        states[block] = result
        part, place = divmod(block, MEM // PARTS)
        table[part * ROWS : (part + 1) * ROWS, place * LANE : (place + 1) * LANE] = result

    out_copies = [pltpu.make_async_copy(states, states_ref, sent.at[MEM])]
    out_copies[0].start()

    column = lax.broadcasted_iota(jnp.int32, (PART_COLS, LANE), 0).astype(jnp.int16)
    for pair in range(SLOT_ROWS // 2):
        hot, codes = [], []
        for row in (2 * pair, 2 * pair + 1):
            pos = pos_ref[row : row + 1, :]
            place = (pos & (PART_COLS - 1)).astype(jnp.int16)
            hot.append(jnp.where(column == place, jnp.ones((), BF16), jnp.zeros((), BF16)))
            codes.append((pos // PART_COLS) * LAYERS + field_ref[row : row + 1, :])
        found = jnp.dot(table[...], jnp.concatenate(hot, axis=1), preferred_element_type=F32)
        for i in range(2):
            hits = [layer == codes[i] - part * LAYERS for part in range(PARTS)]
            for k in range(OWN):
                total = jnp.zeros((LAYERS, LANE), F32)
                for part in range(PARTS):
                    first = part * ROWS + k * LAYERS
                    total = jnp.where(
                        hits[part],
                        found[first : first + LAYERS, i * LANE : (i + 1) * LANE],
                        total,
                    )
                at = k * SLOT_ROWS + 2 * pair + i
                seen[at : at + 1, :] = jnp.sum(total, axis=0, keepdims=True)
    rounded[...] = seen[...].astype(BF16)
    for device in range(MEM):
        copy = pltpu.make_async_copy(rounded, seen_ref.at[device], sent.at[device])
        copy.start()
        out_copies.append(copy)
    for copy in out_copies:
        copy.wait()


def sums_kernel(
    seen_ref, own_ref, near_ref, far_ref, value_ref, base_ref,
    own_sum, near_sum, far_sum, wide, terms, scaled,
):
    weights = (own_ref, near_ref.at[0], near_ref.at[1], far_ref.at[0], far_ref.at[1])
    wide[...] = seen_ref[...].reshape(MEMBERS * SLOT_ROWS, LANE).astype(F32)
    obs_value, base = value_ref[...], base_ref[...]
    first_row = lax.broadcasted_iota(jnp.int32, (16, LANE), 0) == 0
    for row in range(SLOT_ROWS):
        lanes = slice(row * LANE, (row + 1) * LANE)
        values = wide[pl.ds(row, MEMBERS, stride=SLOT_ROWS), :]
        mean = jnp.sum(values, axis=0, keepdims=True) * (1.0 / MEMBERS)
        deviation = values - mean
        terms[0:MEMBERS, lanes] = deviation.astype(BF16)
        innovation = obs_value[row : row + 1, :] - mean
        terms[MEMBERS:, lanes] = jnp.where(first_row, innovation, 0.0).astype(BF16)
        for j in range(5):
            rinv = base[row : row + 1, :] * weights[j][row : row + 1, :]
            scaled[j * MEMBERS : (j + 1) * MEMBERS, lanes] = (deviation * rinv).astype(BF16)
    last = (((1,), (1,)), ((), ()))
    sums = lax.dot_general(terms[...], scaled[...], last, preferred_element_type=F32)
    left = lax.broadcasted_iota(jnp.int32, (32, LANE), 1) < MEMBERS
    outs = (own_sum, near_sum.at[0], near_sum.at[1], far_sum.at[0], far_sum.at[1])
    for j, out in enumerate(outs):
        first = j // 2 * LANE
        part = sums[:, first : min(first + LANE, 5 * MEMBERS)]
        if j == 4:
            part = jnp.concatenate([part, part], axis=1)
        turned = pltpu.roll(part, MEMBERS, 1)
        direct, moved = (part, turned) if j % 2 == 0 else (turned, part)
        out[0:32, :] = jnp.where(left, direct[0:32, :], moved[32:64, :])
        out[32:40, :] = direct[64:72, :]


def regroup_kernel(states_ref, out_ref, wide):
    wide[...] = states_ref[...].reshape(MEM * ROWS, LANE).astype(F32)
    for layer in range(LAYERS):
        out_ref[:, layer * LANE : (layer + 1) * LANE] = wide[
            pl.ds(layer, MEMBERS, stride=LAYERS), :
        ].astype(BF16)


def split(value):
    high = value.astype(BF16)
    return high, (value - high.astype(F32)).astype(BF16)


def split_dot(a, b):
    a_high, a_low = split(a)
    b_high, b_low = split(b)
    left = jnp.concatenate([a_high, a_high, a_low], axis=1)
    right = jnp.concatenate([b_high, b_low, b_high], axis=0)
    return jnp.dot(left, right, preferred_element_type=F32)


def update_kernel(own_ref, far_ref, near_ref, rest_ref, states_ref, land_ref, out_ref, wide):
    block = lax.axis_index("mem")
    total = own_ref[...] + near_ref[0] + far_ref[0] + rest_ref[...]
    total = total * (1.0 / (MEMBERS - 1.0))
    upper = total[0:32, :]
    spread = jnp.concatenate([upper, pltpu.roll(upper, MEMBERS, 1)], axis=0)[:, :MEMBERS]
    pull = total[32:40, :MEMBERS]

    rows = lax.broadcasted_iota(jnp.int32, (MEMBERS, MEMBERS), 0)
    cols = lax.broadcasted_iota(jnp.int32, (MEMBERS, MEMBERS), 1)
    identity = jnp.where(rows == cols, 1.0, 0.0)
    system = identity + spread
    square = jnp.sum(jnp.sum(system * system, axis=1, keepdims=True), axis=0, keepdims=True)
    inv_scale = lax.rsqrt(square)
    current = system * inv_scale
    root = 1.5 * identity - 0.5 * current
    current = split_dot(current, root)
    for sweep in range(1, NS_ITERS):
        middle = 1.5 * identity - 0.5 * split_dot(root, current)
        if sweep < NS_ITERS - 1:
            current = split_dot(current, middle)
        else:
            pull = split_dot(split_dot(pull, root), middle)
        root = split_dot(middle, root)
    mean_weight = split_dot(pull, root)[0:1, :] * inv_scale
    inv_root = root * jnp.sqrt(inv_scale)
    turned = inv_root + mean_weight
    turned = turned + (1.0 - jnp.sum(turned, axis=1, keepdims=True)) * (1.0 / MEMBERS)
    both = jnp.concatenate(split(turned), axis=0)
    land = jnp.broadcast_to(land_ref[pl.ds(block, 1), :], (MEMBERS, LANE)) > 0
    moved = jnp.dot(both, states_ref[...], preferred_element_type=F32)
    for layer in range(LAYERS):
        lanes = slice(layer * LANE, (layer + 1) * LANE)
        result = jnp.where(
            land,
            moved[:MEMBERS, lanes] + moved[MEMBERS:, lanes],
            states_ref[:, lanes].astype(F32),
        )
        wide[pl.ds(layer, MEMBERS, stride=LAYERS), :] = result
    out_ref[...] = wide[...].astype(BF16).reshape(MEM, ROWS, LANE)


def shape(*dims, dtype=BF16):
    return jax.ShapeDtypeStruct(dims, dtype)


def to_tile(value, steps):
    mem, tiles = lax.axis_size("mem"), lax.axis_size("tile")
    pairs = [
        (m * tiles + t, m * tiles + (t + (steps if m % 2 else -steps)) % tiles)
        for m in range(mem)
        for t in range(tiles)
    ]
    return lax.ppermute(value, ("mem", "tile"), pairs)


def to_other_core(value):
    return lax.ppermute(value, "mem", [(m, m ^ 1) for m in range(lax.axis_size("mem"))])


def on_device(
    ensemble_profiles_before,
    mixing_coefficient,
    surface_driver,
    terrain_indicator,
    measured_profile_position,
    measured_field_index,
    obs_valid,
    obs_value,
    obs_error,
    local_weight,
):
    land = terrain_indicator.reshape(MEM, LANE)
    slabs = local_weight.reshape(2 * REACH + 1, SLOT_ROWS, LANE)

    inputs = (
        ensemble_profiles_before,
        mixing_coefficient.reshape(MEM, LANE),
        surface_driver,
        land,
        measured_profile_position.reshape(SLOT_ROWS, LANE),
        measured_field_index.reshape(SLOT_ROWS, LANE),
    )
    states, seen = call(
        forecast_kernel,
        (shape(MEM, ROWS, LANE), shape(MEM, OWN * SLOT_ROWS, LANE)),
        [pltpu.VMEM((PARTS * ROWS, PART_COLS), BF16), pltpu.VMEM((OWN * SLOT_ROWS, LANE), F32)]
        + [pltpu.VMEM((MEM, ROWS, LANE), BF16), pltpu.VMEM((OWN * SLOT_ROWS, LANE), BF16)]
        + [pltpu.VMEM(array.shape, array.dtype) for array in inputs]
        + [pltpu.SemaphoreType.DMA((len(inputs),)), pltpu.SemaphoreType.DMA((MEM + 1,))],
        2 * 4096 * ROWS * 2048,
        2000000,
        *inputs,
        where=pl.ANY,
        vmem=FORECAST_VMEM,
    )
    slabs, obs_value, obs_error, obs_valid, seen = lax.optimization_barrier(
        (slabs, obs_value, obs_error, obs_valid, seen)
    )
    own_weight = slabs[REACH]
    value = obs_value.astype(F32).reshape(SLOT_ROWS, LANE)
    base = (obs_valid.astype(F32) / obs_error.astype(F32)).reshape(SLOT_ROWS, LANE)
    ahead = lax.axis_index("mem") % 2 == 1
    lower, upper = slabs[REACH - 1 :: -1][:REACH], slabs[REACH + 1 :]
    kept, given = jnp.where(ahead, lower, upper), jnp.where(ahead, upper, lower)
    taken = to_other_core(given)
    weights = [
        to_tile(jnp.stack([kept[d - 1], taken[d - 1]]), -d) for d in range(1, REACH + 1)
    ]
    seen = lax.all_to_all(seen, "mem", 0, 0, tiled=True)
    states, seen, taken, own_weight, value, base = lax.optimization_barrier(
        (states, seen, taken, own_weight, value, base)
    )
    states = lax.all_to_all(states, "mem", 0, 0, tiled=True)

    sums = call(
        sums_kernel,
        (shape(PACK, LANE, dtype=F32),) + (shape(2, PACK, LANE, dtype=F32),) * REACH,
        [
            pltpu.VMEM((MEMBERS * SLOT_ROWS, LANE), F32),
            pltpu.VMEM((MEMBERS + 16, SLOT_ROWS * LANE), BF16),
            pltpu.VMEM((5 * MEMBERS, SLOT_ROWS * LANE), BF16),
        ],
        SUMS_FLOPS,
        1000000,
        seen,
        own_weight,
        *weights,
        value,
        base,
    )
    own = sums[0]
    far = to_tile(sums[2], 2)
    near = to_tile(sums[1], 1)
    rest = to_other_core(far[1] + near[1])
    states = call(
        regroup_kernel,
        shape(MEMBERS, LAYERS * LANE),
        [pltpu.VMEM((MEM * ROWS, LANE), F32)],
        MEM * ROWS * LANE,
        1300000,
        states,
    )
    analysed = call(
        update_kernel,
        shape(MEM, ROWS, LANE),
        [pltpu.VMEM((MEM * ROWS, LANE), F32)],
        2 * 128 * 64 * 5120,
        1300000,
        own,
        far,
        near,
        rest,
        states,
        land,
    )
    analysed = lax.all_to_all(analysed, "mem", 0, 0, tiled=True)
    return (
        analysed.reshape(MEM, OWN, LAYERS, LANE)
        .transpose(1, 2, 0, 3)
        .reshape(OWN, LAYERS, MEM * LANE)
    )


def solution(mesh):
    in_specs = (
        P("mem", None, "tile"),
        P("tile"),
        P("mem", "tile"),
        P("tile"),
        P("tile"),
        P("tile"),
        P("tile"),
        P("tile"),
        P("tile"),
        P("mem", "tile", None),
    )
    out_specs = P("mem", None, "tile")
    return jax.shard_map(
        on_device, mesh=mesh, in_specs=in_specs, out_specs=out_specs, check_vma=False
    )
```

```python
import jax
import jax.numpy as jnp
from jax import lax
from jax.experimental import pallas as pl
from jax.experimental.pallas import tpu as pltpu
from jax.sharding import PartitionSpec as P

REACH = 2
NS_ITERS = 3

F32 = jnp.float32
BF16 = jnp.bfloat16
VMEM_LIMIT = 40 * 1024 * 1024
SUMS_FLOPS = 60_000_000_000
FORECAST_VMEM = 62 * 1024 * 1024

MEM = 16
OWN = 4
LAYERS = 40
LANE = 128
ROWS = OWN * LAYERS
MEMBERS = MEM * OWN
PARTS = 4
PART_COLS = 2048 // PARTS
SLOT_ROWS = 32
PACK = 40


def call(kernel, out_shape, scratch, flops, nbytes, *args, where=pltpu.VMEM, vmem=VMEM_LIMIT):
    block = pl.BlockSpec(memory_space=where)
    return pl.pallas_call(
        kernel,
        out_shape=out_shape,
        in_specs=[block] * len(args),
        out_specs=jax.tree.map(lambda _: block, out_shape),
        scratch_shapes=scratch,
        compiler_params=pltpu.CompilerParams(vmem_limit_bytes=vmem),
        cost_estimate=pl.CostEstimate(flops=flops, bytes_accessed=nbytes, transcendentals=0),
    )(*args)


def forecast_kernel(*refs):
    sources, (states_ref, seen_ref, table, seen, states, rounded, *buffers, done, sent) = refs[:6], refs[6:]
    copies = [
        pltpu.make_async_copy(source, buffer, done.at[i])
        for i, (source, buffer) in enumerate(zip(sources, buffers))
    ]
    for copy in copies:
        copy.start()
    for copy in copies:
        copy.wait()
    x_ref, mix_ref, drive_ref, land_ref, pos_ref, field_ref = buffers
    layer = lax.broadcasted_iota(jnp.int32, (LAYERS, LANE), 0)
    for block in range(MEM):
        lanes = slice(block * LANE, (block + 1) * LANE)
        mix = mix_ref[block : block + 1, :]
        land = jnp.broadcast_to(land_ref[block : block + 1, :], (LAYERS, LANE)) > 0
        members = []
        for k in range(OWN):
            x = x_ref[k, :, lanes].astype(F32)
            above = jnp.where(layer == 0, x, pltpu.roll(x, 1, 0))
            below = jnp.where(layer == LAYERS - 1, x, pltpu.roll(x, LAYERS - 1, 0))
            stepped = x + mix * (above - 2.0 * x + below) - 0.05 * x * x * x
            stepped = jnp.where(layer == 0, stepped + drive_ref[k : k + 1, lanes], stepped)
            members.append(jnp.where(land, stepped, x))
        result = jnp.concatenate(members, axis=0).astype(BF16)
        states[block] = result
        part, place = divmod(block, MEM // PARTS)
        table[part * ROWS : (part + 1) * ROWS, place * LANE : (place + 1) * LANE] = result

    out_copies = [pltpu.make_async_copy(states, states_ref, sent.at[MEM])]
    out_copies[0].start()

    column = lax.broadcasted_iota(jnp.int32, (PART_COLS, LANE), 0).astype(jnp.int16)
    for pair in range(SLOT_ROWS // 2):
        hot, codes = [], []
        for row in (2 * pair, 2 * pair + 1):
            pos = pos_ref[row : row + 1, :]
            place = (pos & (PART_COLS - 1)).astype(jnp.int16)
            hot.append(jnp.where(column == place, jnp.ones((), BF16), jnp.zeros((), BF16)))
            codes.append((pos // PART_COLS) * LAYERS + field_ref[row : row + 1, :])
        found = jnp.dot(table[...], jnp.concatenate(hot, axis=1), preferred_element_type=F32)
        for i in range(2):
            hits = [layer == codes[i] - part * LAYERS for part in range(PARTS)]
            for k in range(OWN):
                total = jnp.zeros((LAYERS, LANE), F32)
                for part in range(PARTS):
                    first = part * ROWS + k * LAYERS
                    total = jnp.where(
                        hits[part],
                        found[first : first + LAYERS, i * LANE : (i + 1) * LANE],
                        total,
                    )
                at = k * SLOT_ROWS + 2 * pair + i
                seen[at : at + 1, :] = jnp.sum(total, axis=0, keepdims=True)
    rounded[...] = seen[...].astype(BF16)
    for device in range(MEM):
        copy = pltpu.make_async_copy(rounded, seen_ref.at[device], sent.at[device])
        copy.start()
        out_copies.append(copy)
    for copy in out_copies:
        copy.wait()


def sums_kernel(
    seen_ref, own_ref, near_ref, far_ref, value_ref, base_ref,
    own_sum, near_sum, far_sum, wide, terms, scaled,
):
    weights = (own_ref, near_ref.at[0], near_ref.at[1], far_ref.at[0], far_ref.at[1])
    wide[...] = seen_ref[...].reshape(MEMBERS * SLOT_ROWS, LANE).astype(F32)
    obs_value, base = value_ref[...], base_ref[...]
    first_row = lax.broadcasted_iota(jnp.int32, (16, LANE), 0) == 0
    for row in range(SLOT_ROWS):
        lanes = slice(row * LANE, (row + 1) * LANE)
        values = wide[pl.ds(row, MEMBERS, stride=SLOT_ROWS), :]
        mean = jnp.sum(values, axis=0, keepdims=True) * (1.0 / MEMBERS)
        deviation = values - mean
        terms[0:MEMBERS, lanes] = deviation.astype(BF16)
        innovation = obs_value[row : row + 1, :] - mean
        terms[MEMBERS:, lanes] = jnp.where(first_row, innovation, 0.0).astype(BF16)
        for j in range(5):
            rinv = base[row : row + 1, :] * weights[j][row : row + 1, :]
            scaled[j * MEMBERS : (j + 1) * MEMBERS, lanes] = (deviation * rinv).astype(BF16)
    last = (((1,), (1,)), ((), ()))
    sums = lax.dot_general(terms[...], scaled[...], last, preferred_element_type=F32)
    left = lax.broadcasted_iota(jnp.int32, (32, LANE), 1) < MEMBERS
    outs = (own_sum, near_sum.at[0], near_sum.at[1], far_sum.at[0], far_sum.at[1])
    for j, out in enumerate(outs):
        first = j // 2 * LANE
        part = sums[:, first : min(first + LANE, 5 * MEMBERS)]
        if j == 4:
            part = jnp.concatenate([part, part], axis=1)
        turned = pltpu.roll(part, MEMBERS, 1)
        direct, moved = (part, turned) if j % 2 == 0 else (turned, part)
        out[0:32, :] = jnp.where(left, direct[0:32, :], moved[32:64, :])
        out[32:40, :] = direct[64:72, :]


def split(value):
    high = value.astype(BF16)
    return high, (value - high.astype(F32)).astype(BF16)


def split_dot(a, b):
    a_high, a_low = split(a)
    b_high, b_low = split(b)
    left = jnp.concatenate([a_high, a_high, a_low], axis=1)
    right = jnp.concatenate([b_high, b_low, b_high], axis=0)
    return jnp.dot(left, right, preferred_element_type=F32)


def update_kernel(own_ref, far_ref, near_ref, rest_ref, received_ref, land_ref, out_ref, wide, states_ref):
    wide[...] = received_ref[...].reshape(MEM * ROWS, LANE).astype(F32)
    for layer in range(LAYERS):
        states_ref[:, layer * LANE : (layer + 1) * LANE] = wide[
            pl.ds(layer, MEMBERS, stride=LAYERS), :
        ].astype(BF16)
    block = lax.axis_index("mem")
    total = own_ref[...] + near_ref[0] + far_ref[0] + rest_ref[...]
    total = total * (1.0 / (MEMBERS - 1.0))
    upper = total[0:32, :]
    spread = jnp.concatenate([upper, pltpu.roll(upper, MEMBERS, 1)], axis=0)[:, :MEMBERS]
    pull = total[32:40, :MEMBERS]

    rows = lax.broadcasted_iota(jnp.int32, (MEMBERS, MEMBERS), 0)
    cols = lax.broadcasted_iota(jnp.int32, (MEMBERS, MEMBERS), 1)
    identity = jnp.where(rows == cols, 1.0, 0.0)
    system = identity + spread
    square = jnp.sum(jnp.sum(system * system, axis=1, keepdims=True), axis=0, keepdims=True)
    inv_scale = lax.rsqrt(square)
    current = system * inv_scale
    root = 1.5 * identity - 0.5 * current
    current = split_dot(current, root)
    for sweep in range(1, NS_ITERS):
        middle = 1.5 * identity - 0.5 * split_dot(root, current)
        if sweep < NS_ITERS - 1:
            current = split_dot(current, middle)
        else:
            pull = split_dot(split_dot(pull, root), middle)
        root = split_dot(middle, root)
    mean_weight = split_dot(pull, root)[0:1, :] * inv_scale
    inv_root = root * jnp.sqrt(inv_scale)
    turned = inv_root + mean_weight
    turned = turned + (1.0 - jnp.sum(turned, axis=1, keepdims=True)) * (1.0 / MEMBERS)
    both = jnp.concatenate(split(turned), axis=0)
    land = jnp.broadcast_to(land_ref[pl.ds(block, 1), :], (MEMBERS, LANE)) > 0
    moved = jnp.dot(both, states_ref[...], preferred_element_type=F32)
    for layer in range(LAYERS):
        lanes = slice(layer * LANE, (layer + 1) * LANE)
        result = jnp.where(
            land,
            moved[:MEMBERS, lanes] + moved[MEMBERS:, lanes],
            states_ref[:, lanes].astype(F32),
        )
        wide[pl.ds(layer, MEMBERS, stride=LAYERS), :] = result
    out_ref[...] = wide[...].astype(BF16).reshape(MEM, ROWS, LANE)


def shape(*dims, dtype=BF16):
    return jax.ShapeDtypeStruct(dims, dtype)


def to_tile(value, steps):
    mem, tiles = lax.axis_size("mem"), lax.axis_size("tile")
    pairs = [
        (m * tiles + t, m * tiles + (t + (steps if m % 2 else -steps)) % tiles)
        for m in range(mem)
        for t in range(tiles)
    ]
    return lax.ppermute(value, ("mem", "tile"), pairs)


def to_other_core(value):
    return lax.ppermute(value, "mem", [(m, m ^ 1) for m in range(lax.axis_size("mem"))])


def on_device(
    ensemble_profiles_before,
    mixing_coefficient,
    surface_driver,
    terrain_indicator,
    measured_profile_position,
    measured_field_index,
    obs_valid,
    obs_value,
    obs_error,
    local_weight,
):
    land = terrain_indicator.reshape(MEM, LANE)
    slabs = local_weight.reshape(2 * REACH + 1, SLOT_ROWS, LANE)

    inputs = (
        ensemble_profiles_before,
        mixing_coefficient.reshape(MEM, LANE),
        surface_driver,
        land,
        measured_profile_position.reshape(SLOT_ROWS, LANE),
        measured_field_index.reshape(SLOT_ROWS, LANE),
    )
    states, seen = call(
        forecast_kernel,
        (shape(MEM, ROWS, LANE), shape(MEM, OWN * SLOT_ROWS, LANE)),
        [pltpu.VMEM((PARTS * ROWS, PART_COLS), BF16), pltpu.VMEM((OWN * SLOT_ROWS, LANE), F32)]
        + [pltpu.VMEM((MEM, ROWS, LANE), BF16), pltpu.VMEM((OWN * SLOT_ROWS, LANE), BF16)]
        + [pltpu.VMEM(array.shape, array.dtype) for array in inputs]
        + [pltpu.SemaphoreType.DMA((len(inputs),)), pltpu.SemaphoreType.DMA((MEM + 1,))],
        2 * 4096 * ROWS * 2048,
        2000000,
        *inputs,
        where=pl.ANY,
        vmem=FORECAST_VMEM,
    )
    slabs, obs_value, obs_error, obs_valid, seen = lax.optimization_barrier(
        (slabs, obs_value, obs_error, obs_valid, seen)
    )
    own_weight = slabs[REACH]
    value = obs_value.astype(F32).reshape(SLOT_ROWS, LANE)
    base = (obs_valid.astype(F32) / obs_error.astype(F32)).reshape(SLOT_ROWS, LANE)
    ahead = lax.axis_index("mem") % 2 == 1
    lower, upper = slabs[REACH - 1 :: -1][:REACH], slabs[REACH + 1 :]
    kept, given = jnp.where(ahead, lower, upper), jnp.where(ahead, upper, lower)
    taken = to_other_core(given)
    weights = [
        to_tile(jnp.stack([kept[d - 1], taken[d - 1]]), -d) for d in range(1, REACH + 1)
    ]
    seen = lax.all_to_all(seen, "mem", 0, 0, tiled=True)
    states, seen, taken, own_weight, value, base = lax.optimization_barrier(
        (states, seen, taken, own_weight, value, base)
    )
    states = lax.all_to_all(states, "mem", 0, 0, tiled=True)

    sums = call(
        sums_kernel,
        (shape(PACK, LANE, dtype=F32),) + (shape(2, PACK, LANE, dtype=F32),) * REACH,
        [
            pltpu.VMEM((MEMBERS * SLOT_ROWS, LANE), F32),
            pltpu.VMEM((MEMBERS + 16, SLOT_ROWS * LANE), BF16),
            pltpu.VMEM((5 * MEMBERS, SLOT_ROWS * LANE), BF16),
        ],
        SUMS_FLOPS,
        1000000,
        seen,
        own_weight,
        *weights,
        value,
        base,
    )
    own = sums[0]
    far = to_tile(sums[2], 2)
    near = to_tile(sums[1], 1)
    rest = to_other_core(far[1] + near[1])
    analysed = call(
        update_kernel,
        shape(MEM, ROWS, LANE),
        [pltpu.VMEM((MEM * ROWS, LANE), F32), pltpu.VMEM((MEMBERS, LAYERS * LANE), BF16)],
        2 * 128 * 64 * 5120,
        1300000,
        own,
        far,
        near,
        rest,
        states,
        land,
    )
    analysed = lax.all_to_all(analysed, "mem", 0, 0, tiled=True)
    return (
        analysed.reshape(MEM, OWN, LAYERS, LANE)
        .transpose(1, 2, 0, 3)
        .reshape(OWN, LAYERS, MEM * LANE)
    )


def solution(mesh):
    in_specs = (
        P("mem", None, "tile"),
        P("tile"),
        P("mem", "tile"),
        P("tile"),
        P("tile"),
        P("tile"),
        P("tile"),
        P("tile"),
        P("tile"),
        P("mem", "tile", None),
    )
    out_specs = P("mem", None, "tile")
    return jax.shard_map(
        on_device, mesh=mesh, in_specs=in_specs, out_specs=out_specs, check_vma=False
    )
```
